32 devices in a mesh: band: 8 (over y, x, core), req: 4 (over z).
Axes of the slice: x: 2, y: 2, z: 4, core: 2. Of those that a mesh axis runs over, the one named last changes fastest.
Arguments:
- latents: bfloat16 [4, 32, 512, 320], P('req', 'band'), may hold values from -40 to 40
- request_time_embedding: bfloat16 [4, 1280], P('req'), may hold values from -6 to 6
- request_adapter: int32 [4, 1], P('req'), may hold values from 0 to 31, as said below
- adapter_stored_row: int32 [32], replicated, may hold values from 0 to 31, as said below
- first_conv_weight: bfloat16 [3, 3, 320, 320], replicated, may hold values from -0.109375 to 0.109375
- stored_down_weight: bfloat16 [32, 3, 3, 320, 64], P(('band', 'req')), may hold values from -0.109375 to 0.109375
- stored_up_weight: bfloat16 [32, 64, 320], P(('band', 'req')), may hold values from -0.75 to 0.75
- second_conv_weight: bfloat16 [3, 3, 320, 320], replicated, may hold values from -0.109375 to 0.109375
- time_projection_weight: bfloat16 [1280, 320], replicated, may hold values from -0.15625 to 0.15625
Outputs:
- block_out: bfloat16 [4, 32, 512, 320], P('req', 'band')
The draws below stay inside these ranges and needn't reach their ends.
Inputs may be any that keep to these rules, and one draw needn't show every extreme that they name: `request_adapter`: ids of adapters. `adapter_stored_row`: each stored row appears once.
All inputs are finite; a program needn't handle non-finite values.
Results may differ from the reference program's by a relative error of at most 0.0038.
Values may be sent and summed in bfloat16 or wider, within the bound.
A program may use at most 128 MiB of HBM per device.

```python
import jax
import jax.numpy as jnp
from jax import lax

CHANNEL_COUNT = 320
G = 32
TD = 1280
ADAPTER_RANK = 64
W = 512
ADAPT_DEV = 1
REQ_DEV = 1
H = 32
REQUESTS = 4
ADAPTER_TOTAL = 32


def draw_latents(key, part):
    key_base = jax.random.fold_in(key, 11)
    key_chan = jax.random.fold_in(key, 12)
    base = jnp.clip(jax.random.normal(key_base, (REQUESTS, H, W, CHANNEL_COUNT), jnp.float32), -6.0, 6.0)
    position = jnp.arange(H, dtype=jnp.float32) / max(H - 1, 1)
    row_scale = 0.5 + position
    chan_scale = jnp.exp(jax.random.uniform(key_chan, (CHANNEL_COUNT,), jnp.float32, jnp.log(0.5), jnp.log(2.0)))
    values = base * row_scale[None, :, None, None] * chan_scale[None, None, None, :]
    return values.astype(jnp.bfloat16)


def stored_order(key):
    return jax.random.permutation(jax.random.fold_in(key, 7), ADAPTER_TOTAL).astype(jnp.int32)


def draw_adapter_stored_row(key, part):
    return stored_order(key)


def draw_request_adapter(key, part):
    order = stored_order(key)
    inverse = jnp.argsort(order).astype(jnp.int32)
    req_count = REQUESTS // REQ_DEV
    band_count = ADAPTER_TOTAL // (ADAPT_DEV * req_count)
    request_ids = jnp.arange(REQUESTS, dtype=jnp.int32)
    own_req = request_ids // REQ_DEV
    random_req = jax.random.randint(jax.random.fold_in(key, 21), (REQUESTS,), 0, req_count, jnp.int32)
    far_req = (own_req + req_count // 2) % req_count
    target_req = jnp.where(request_ids % 2 == 0, far_req, random_req)
    target_band = jax.random.randint(jax.random.fold_in(key, 22), (REQUESTS,), 0, band_count, jnp.int32)
    local_slot = jax.random.randint(jax.random.fold_in(key, 23), (REQUESTS,), 0, ADAPT_DEV, jnp.int32)
    stored = (target_band * req_count + target_req) * ADAPT_DEV + local_slot
    ids = inverse[stored]
    ids = jnp.where(request_ids == 0, jnp.int32(ADAPTER_TOTAL - 1), ids)
    ids = jnp.where(request_ids == 1, jnp.int32(0), ids)
    return ids.astype(jnp.int32).reshape(REQUESTS, 1)


def shard_levels(stream_key, shape, split, low, high):
    gain = 1.0
    for dim, shards_of in split:
        steps = jax.random.uniform(jax.random.fold_in(jax.random.fold_in(stream_key, 6), dim), (shards_of,), jnp.float32, low / len(split), high / len(split))
        gain = gain * jnp.repeat(jnp.exp(steps), shape[dim] // shards_of).reshape((-1,) + (1,) * (len(shape) - 1 - dim))
    return gain


def scatter_about(key, dims, width, limit, shards=(), kind=jnp.bfloat16):
    values = jax.random.normal(key, dims, jnp.float32) * width
    if len(shards) > 0:
        values = shard_levels(key, dims, shards, -0.22, 0.18) * values
    return jnp.clip(values, min=-limit, max=limit).astype(kind)


def setup_inputs(seed: int = 0) -> dict:
    key_list = jax.random.split(jax.random.key(seed), 10)
    latents = draw_latents(jax.random.fold_in(key_list[9], 71), 0)
    request_time_embedding = scatter_about(key_list[1], (REQUESTS, TD), 1.0, 6.0, ((0, 4),))
    request_adapter = draw_request_adapter(jax.random.fold_in(key_list[9], 71), 0)
    adapter_stored_row = draw_adapter_stored_row(jax.random.fold_in(key_list[9], 71), 0)
    first_conv_weight = scatter_about(key_list[4], (3, 3, CHANNEL_COUNT, CHANNEL_COUNT), (9 * CHANNEL_COUNT) ** -0.5, 0.109375)
    stored_down_weight = scatter_about(key_list[5], (ADAPTER_TOTAL, 3, 3, CHANNEL_COUNT, ADAPTER_RANK), (9 * CHANNEL_COUNT) ** -0.5, 0.109375, ((0, 32),))
    stored_up_weight = scatter_about(key_list[6], (ADAPTER_TOTAL, ADAPTER_RANK, CHANNEL_COUNT), ADAPTER_RANK ** -0.5, 0.75, ((0, 32),))
    second_conv_weight = scatter_about(key_list[7], (3, 3, CHANNEL_COUNT, CHANNEL_COUNT), (9 * CHANNEL_COUNT) ** -0.5, 0.109375)
    time_projection_weight = scatter_about(key_list[8], (TD, CHANNEL_COUNT), TD ** -0.5, 0.15625)
    return {"latents": latents, "request_time_embedding": request_time_embedding, "request_adapter": request_adapter, "adapter_stored_row": adapter_stored_row, "first_conv_weight": first_conv_weight, "stored_down_weight": stored_down_weight, "stored_up_weight": stored_up_weight, "second_conv_weight": second_conv_weight, "time_projection_weight": time_projection_weight}


def group_norm(field):
    grouped = field.reshape(H, W, G, CHANNEL_COUNT // G)
    center = lax.optimization_barrier(jnp.mean(grouped, axis=(0, 1, 3), keepdims=True))
    spread = lax.optimization_barrier(jnp.mean((grouped - center) ** 2, axis=(0, 1, 3), keepdims=True))
    return ((grouped - center) * lax.rsqrt(spread + 1e-05)).reshape(H, W, CHANNEL_COUNT)

def convolve(padded, kernel):
    total = None
    for row_tap in range(3):
        for col_tap in range(3):
            term = jnp.einsum('hwc,cd->hwd', padded[row_tap:row_tap + H, col_tap:col_tap + W], kernel[row_tap, col_tap].astype(jnp.float32))
            total = term if total is None else total + term
    return total

def pad_field(field):
    return jnp.pad(field.astype(jnp.float32), ((1, 1), (1, 1), (0, 0)))

def reference(latents, request_time_embedding, request_adapter, adapter_stored_row, first_conv_weight, stored_down_weight, stored_up_weight, second_conv_weight, time_projection_weight):
    shifts = jnp.dot(jax.nn.silu(request_time_embedding.astype(jnp.float32)).astype(jnp.bfloat16), time_projection_weight, preferred_element_type=jnp.float32)

    def one_request(items):
        image, chosen, shift = items
        stored_index = adapter_stored_row[chosen[0]]
        down_matrix = lax.dynamic_index_in_dim(stored_down_weight, stored_index, 0, keepdims=False)
        up_matrix = lax.dynamic_index_in_dim(stored_up_weight, stored_index, 0, keepdims=False)
        first = jax.nn.silu(group_norm(image.astype(jnp.float32))).astype(jnp.bfloat16)
        padded = pad_field(first)
        main = convolve(padded, first_conv_weight)
        lowrank = convolve(padded, down_matrix).astype(jnp.bfloat16)
        lifted = jnp.dot(lowrank.reshape(H * W, ADAPTER_RANK), up_matrix, preferred_element_type=jnp.float32).reshape(H, W, CHANNEL_COUNT)
        hidden = main + lifted + shift[None, None, :]
        second = jax.nn.silu(group_norm(hidden)).astype(jnp.bfloat16)
        result = image.astype(jnp.float32) + convolve(pad_field(second), second_conv_weight)
        return result.astype(jnp.bfloat16)
    return lax.map(one_request, (latents, request_adapter, shifts))
```

```python
import functools

import jax
import jax.numpy as jnp
import numpy as np
from jax import lax
from jax.experimental import pallas as pl
from jax.experimental.pallas import tpu as pltpu
from jax.sharding import PartitionSpec as P

G = 32
EPS = 1e-05
MESH = pl.DeviceIdType.MESH
F32 = jnp.float32
BF16 = jnp.bfloat16
LANES = 128
CHUNK = 64


def round_up(value, step):
    return -(-value // step) * step


def split3(v):
    hi = v.astype(BF16)
    rest = v - hi.astype(F32)
    mid = rest.astype(BF16)
    return hi, mid, (rest - mid.astype(F32)).astype(BF16)


def kernel(
    dims,
    lat_ref, temb_ref, ra_ref, row_ref, w1_hbm, down_hbm, up_hbm, w2_hbm, tp_hbm, gg_ref,
    out_ref,
    lat, act, x, hid, w1, w2, rhs2, up_pad, tp, down, up, shift,
    stat1, stat2, slots, packed, recv1, sel, recv2, full,
    hsend, hrecv, musend, murecv, outbuf,
    ld_sem, w1_sem, w2_sem, out_sem,
    s1s, s1r, s2s, s2r, sls, slr, p1s, p1r, p2s, p2r, p3s, p3r, has, har, hbs, hbr, hms, hmr,
):
    B, R, rows, width, C, rank, piece = dims
    CP = round_up(C, LANES)
    count = rows * width
    me = lax.axis_index("band")
    mr = lax.axis_index("req")
    half = 9 * C // 2

    def band(d):
        return lax.rem(me + d, B)

    def req(e):
        return lax.rem(mr + e, R)

    ld = [
        pltpu.make_async_copy(lat_ref.at[0], lat.at[pl.ds(1, rows)], ld_sem.at[0]),
        pltpu.make_async_copy(down_hbm.at[0], down, ld_sem.at[1]),
        pltpu.make_async_copy(up_hbm.at[0], up, ld_sem.at[2]),
        pltpu.make_async_copy(tp_hbm, tp, ld_sem.at[3]),
    ]
    for copy in ld:
        copy.start()

    def weight_copies(src, dst, sems):
        copies = []
        for i in range(3):
            for j in range(3):
                k = (i * 3 + j) * 2
                copies.append(pltpu.make_async_copy(
                    src.at[i, j, pl.ds(0, 256)], dst.at[i, pl.ds(256 * j, 256)], sems.at[k]))
                copies.append(pltpu.make_async_copy(
                    src.at[i, j, pl.ds(256, 64)], dst.at[i, pl.ds(768 + 64 * j, 64)], sems.at[k + 1]))
        return copies

    w1_copies = weight_copies(w1_hbm, w1, w1_sem)
    w2_copies = weight_copies(w2_hbm, w2, w2_sem)
    for copy in w1_copies + w2_copies:
        copy.start()

    barrier = pltpu.get_barrier_semaphore()
    for d in range(1, B):
        pl.semaphore_signal(barrier, inc=1, device_id={"band": band(d)}, device_id_type=MESH)
    for e in range(1, R):
        pl.semaphore_signal(barrier, inc=1, device_id={"req": req(e)}, device_id_type=MESH)

    slot = row_ref[ra_ref[0, 0]]
    slots[0] = jnp.full((8, LANES), slot, jnp.int32)
    ld[1].wait()
    ld[2].wait()
    flat = packed
    total_rows = half + 3 * rank
    zero64 = jnp.zeros((rank, 64), BF16)
    for start in range(0, half, 160):
        t0, c0 = start // C, start % C
        t1, c1 = (start + half) // C, (start + half) % C
        flat[pl.ds(start, 160), :] = jnp.concatenate(
            [down[t0 // 3, t0 % 3, pl.ds(c0, 160), :], down[t1 // 3, t1 % 3, pl.ds(c1, 160), :]], axis=1)
    flat[pl.ds(half, rank), :] = up[:, 0:128]
    flat[pl.ds(half + rank, rank), :] = up[:, 128:256]
    flat[pl.ds(half + 2 * rank, rank), :] = jnp.concatenate([up[:, 256:320], zero64], axis=1)
    pad_rows = B * piece - total_rows
    if pad_rows:
        flat[pl.ds(total_rows, pad_rows), :] = jnp.zeros((pad_rows, LANES), BF16)

    ld[0].wait()
    shift[...] = jnp.zeros_like(shift)
    stat1[0] = jnp.zeros((8, CP), F32)
    stat2[0] = jnp.zeros((8, CP), F32)

    def lat_sum(k, acc):
        v = lat[1 + k // (width // CHUNK), pl.ds(pl.multiple_of((k % (width // CHUNK)) * CHUNK, CHUNK), CHUNK), :].astype(F32)
        return acc + jnp.sum(v.reshape(CHUNK // 8, 8, C), axis=0)

    steps = rows * (width // CHUNK)
    sums = lax.fori_loop(0, steps, lat_sum, jnp.zeros((8, C), F32))
    mean = jnp.sum(sums, axis=0, keepdims=True) * (1.0 / count)

    def lat_dev(k, acc):
        v = lat[1 + k // (width // CHUNK), pl.ds(pl.multiple_of((k % (width // CHUNK)) * CHUNK, CHUNK), CHUNK), :].astype(F32)
        v = v - mean
        return acc + jnp.sum((v * v).reshape(CHUNK // 8, 8, C), axis=0)

    devs = lax.fori_loop(0, steps, lat_dev, jnp.zeros((8, C), F32))
    stat1[0, 0:1, 0:C] = mean
    stat1[0, 1:2, 0:C] = jnp.sum(devs, axis=0, keepdims=True)

    pl.semaphore_wait(barrier, B - 1 + R - 1)

    def send_stats(buf, ss, rs):
        out = []
        for d in range(1, B):
            out.append(pltpu.make_async_remote_copy(
                src_ref=buf.at[0], dst_ref=buf.at[d], send_sem=ss.at[d], recv_sem=rs.at[d],
                device_id={"band": band(d)}, device_id_type=MESH))
            out[-1].start()
        return out

    stat1_copies = send_stats(stat1, s1s, s1r)
    slot_copies = []
    for e in range(1, R):
        slot_copies.append(pltpu.make_async_remote_copy(
            src_ref=slots.at[0], dst_ref=slots.at[e], send_sem=sls.at[e], recv_sem=slr.at[e],
            device_id={"req": req(e)}, device_id_type=MESH))
        slot_copies[-1].start()

    p1_copies = []
    for d in range(1, B):
        p1_copies.append(pltpu.make_async_remote_copy(
            src_ref=packed.at[pl.ds(pl.multiple_of(band(d) * piece, 16), piece)], dst_ref=recv1.at[d],
            send_sem=p1s.at[d], recv_sem=p1r.at[d], device_id={"band": band(d)}, device_id_type=MESH))
        p1_copies[-1].start()

    def up_copy():
        return pltpu.make_async_remote_copy(
            src_ref=lat.at[1], dst_ref=lat.at[rows + 1], send_sem=has.at[0], recv_sem=har.at[0],
            device_id={"band": lax.rem(me + B - 1, B)}, device_id_type=MESH)

    def down_copy():
        return pltpu.make_async_remote_copy(
            src_ref=lat.at[rows], dst_ref=lat.at[0], send_sem=has.at[1], recv_sem=har.at[1],
            device_id={"band": band(1)}, device_id_type=MESH)

    @pl.when(me > 0)
    def _():
        up_copy().start()

    @pl.when(me < B - 1)
    def _():
        down_copy().start()

    ld[3].wait()
    t = temb_ref[...].astype(F32)
    t = (t / (1.0 + jnp.exp(-t))).astype(BF16).astype(F32)
    t = jnp.broadcast_to(t, (16, t.shape[1])).astype(BF16)
    shift[0:1, 0:C] = jnp.dot(t, tp[...], preferred_element_type=F32)[0:1]

    act[...] = jnp.zeros_like(act)
    for i in range(3):
        w1[i, pl.ds(960, 64), :] = jnp.zeros((64, C), BF16)
        w2[i, pl.ds(960, 64), :] = jnp.zeros((64, C), BF16)
        rhs2[i, pl.ds(960, 64), :] = jnp.zeros((64, LANES), BF16)

    def group_sum(v):
        v = jnp.broadcast_to(v, (16, CP))
        gg = gg_ref[...]
        return sum(jnp.dot(part, gg, preferred_element_type=F32) for part in split3(v))[0:1]

    def combine(buf):
        cpg = C // G
        total = buf[0]
        for d in range(1, B):
            total = total + buf[d]
        m = group_sum(total[0:1]) * (1.0 / (cpg * B))
        dev = jnp.zeros((1, CP), F32)
        for d in range(B):
            diff = buf[d][0:1] - m
            dev = dev + diff * diff
        valid = lax.broadcasted_iota(jnp.int32, (1, CP), 1) < C
        dev = jnp.where(valid, total[1:2] + float(count) * dev, 0.0)
        spread = group_sum(dev) * (1.0 / (float(count) * cpg * B))
        return m, 0.5 * lax.rsqrt(spread + EPS)

    def silu_half(h):
        return h * jnp.tanh(h) + h

    def spread_row(r):
        for c in range(0, width, CHUNK):
            v = act[pl.ds(c, CHUNK + 16), :]
            before = pltpu.roll(v, 1, 0)[8:8 + CHUNK]
            after = pltpu.roll(v, CHUNK + 15, 0)[8:8 + CHUNK]
            here = v[8:8 + CHUNK]
            x[r, pl.ds(c, CHUNK), 0:256] = before[:, 0:256].astype(BF16)
            x[r, pl.ds(c, CHUNK), 256:512] = here[:, 0:256].astype(BF16)
            x[r, pl.ds(c, CHUNK), 512:768] = after[:, 0:256].astype(BF16)
            x[r, pl.ds(c, CHUNK), 768:896] = (before[:, 256:384] + pltpu.roll(here[:, 256:384], 64, 1)).astype(BF16)
            x[r, pl.ds(c, CHUNK), 896:1024] = after[:, 256:384].astype(BF16)

    for copy in stat1_copies:
        copy.wait_recv()
    m1, a1 = combine(stat1)
    m1, a1 = m1[:, 0:C], a1[:, 0:C]

    def first_row(r):
        for c in range(0, width, CHUNK):
            v = lat[r, pl.ds(c, CHUNK), :].astype(F32)
            act[pl.ds(8 + c, CHUNK), 0:C] = silu_half((v - m1) * a1)
        spread_row(r)

    def first_body(k, _):
        first_row(1 + k)
        return 0

    lax.fori_loop(0, rows, first_body, 0)

    for copy in p1_copies + slot_copies:
        copy.wait_recv()
    p2_copies = []
    own = packed[pl.ds(pl.multiple_of(me * piece, 16), piece), :].astype(F32)
    for n in range(R):
        e = (n + 1) % R
        wanted = slots[(R - e) % R][0:1]
        acc = own * (wanted == me * R + mr).astype(F32)
        for d in range(1, B):
            ident = lax.rem(me - d + B, B) * R + mr
            acc = acc + recv1[d].astype(F32) * (wanted == ident).astype(F32)
        sel[e] = acc.astype(BF16)
        if e:
            p2_copies.append(pltpu.make_async_remote_copy(
                src_ref=sel.at[e], dst_ref=recv2.at[e], send_sem=p2s.at[e], recv_sem=p2r.at[e],
                device_id={"req": req(e)}, device_id_type=MESH))
            p2_copies[-1].start()

    zero_row = jnp.zeros((width, 1024), BF16)

    @pl.when(me > 0)
    def _():
        down_copy().wait_recv()
        first_row(0)

    @pl.when(me == 0)
    def _():
        x[0] = zero_row

    @pl.when(me < B - 1)
    def _():
        up_copy().wait_recv()
        first_row(rows + 1)

    @pl.when(me == B - 1)
    def _():
        x[rows + 1] = zero_row

    for copy in w1_copies:
        copy.wait()

    def conv(r, weights, lo, hi):
        total = None
        for i in range(3):
            term = jnp.dot(x[r + i], weights[i, :, lo:hi], preferred_element_type=F32)
            total = term if total is None else total + term
        return total

    def main_body(r, _):
        hid[r, :, 0:256] = conv(r, w1, 0, 256) + shift[0:1, 0:256]
        return 0

    lax.fori_loop(0, 1, main_body, 0)

    for copy in p2_copies:
        copy.wait_recv()
    acc = sel[0].astype(F32)
    for e in range(1, R):
        acc = acc + recv2[e].astype(F32)
    full[me] = acc.astype(BF16)
    p3_copies = []
    for d in range(1, B):
        p3_copies.append(pltpu.make_async_remote_copy(
            src_ref=full.at[me], dst_ref=full.at[me], send_sem=p3s.at[d], recv_sem=p3r.at[d],
            device_id={"band": band(d)}, device_id_type=MESH))
        p3_copies[-1].start()

    lax.fori_loop(1, rows, main_body, 0)

    for d in range(1, B):
        pltpu.make_async_remote_copy(
            src_ref=full.at[me], dst_ref=full.at[lax.rem(me - d + B, B)], send_sem=p3s.at[d], recv_sem=p3r.at[d],
            device_id={"band": band(d)}, device_id_type=MESH).wait_recv()

    low_lane = lax.broadcasted_iota(jnp.int32, (1, LANES), 1) < 64

    def adapter_rows(start, size):
        parts = []
        while size:
            p, o = start // piece, start % piece
            take = min(size, piece - o)
            parts.append(full[p, pl.ds(o, take), :].astype(F32))
            start, size = start + take, size - take
        return parts[0] if len(parts) == 1 else jnp.concatenate(parts, axis=0)

    def place(i, k, start, size):
        main3 = w1[i, pl.ds(k, size), 256:320].astype(F32)
        main3 = jnp.concatenate([main3, jnp.zeros((size, 64), F32)], axis=1)
        if start < half:
            v = pltpu.roll(adapter_rows(start, size), 64, 1)
        else:
            v = adapter_rows(start - half, size)
        rhs2[i, pl.ds(k, size), :] = jnp.where(low_lane, main3, v).astype(BF16)

    for i in range(3):
        for j in range(3):
            base = (i * 3 + j) * C
            for c in range(0, C, 32):
                k = 256 * j + c if c < 256 else 768 + 64 * j + c - 256
                place(i, k, base + c, 32)
    up_pad[pl.ds(0, 64), :] = jnp.zeros((64, CP), BF16)
    for b in range(3):
        up_pad[pl.ds(64, rank), 128 * b:128 * b + 128] = adapter_rows(half + b * rank, rank).astype(BF16)

    def hidden_row(r):
        t = conv(r, rhs2, 0, 128)
        lifted = jnp.dot(t.astype(BF16), up_pad[...], preferred_element_type=F32)
        hid[r, :, 0:256] = hid[r, :, 0:256] + lifted[:, 0:256]
        hid[r, :, 256:384] = jnp.where(low_lane, t, 0.0) + lifted[:, 256:384] + shift[0:1, 256:384]

    def row_chunk(r, c):
        return hid[r, pl.ds(c, CHUNK), :]

    def row_sum(r):
        acc = jnp.zeros((8, CP), F32)
        for c in range(0, width, CHUNK):
            acc = acc + jnp.sum(row_chunk(r, c).reshape(CHUNK // 8, 8, CP), axis=0)
        return jnp.sum(acc, axis=0, keepdims=True)

    def edge_body(k, acc):
        r = k * (rows - 1)
        hidden_row(r)
        total = row_sum(r)
        mu = total * (1.0 / width)
        musend[k] = jnp.broadcast_to(mu, (8, CP))
        for c in range(0, width, CHUNK):
            hsend[k, pl.ds(c, CHUNK), :] = (row_chunk(r, c) - mu).astype(BF16)
        return acc + total

    def halo_copies(k):
        target = lax.rem(me + B - 1, B) if k == 0 else band(1)
        return (
            pltpu.make_async_remote_copy(
                src_ref=hsend.at[k], dst_ref=hrecv.at[1 - k], send_sem=hbs.at[k], recv_sem=hbr.at[k],
                device_id={"band": target}, device_id_type=MESH),
            pltpu.make_async_remote_copy(
                src_ref=musend.at[k], dst_ref=murecv.at[1 - k], send_sem=hms.at[k], recv_sem=hmr.at[k],
                device_id={"band": target}, device_id_type=MESH),
        )

    total = lax.fori_loop(0, 2, edge_body, jnp.zeros((1, CP), F32))

    @pl.when(me > 0)
    def _():
        for copy in halo_copies(0):
            copy.start()

    @pl.when(me < B - 1)
    def _():
        for copy in halo_copies(1):
            copy.start()

    def inner_body(r, acc):
        hidden_row(r)
        return acc + row_sum(r)

    total = lax.fori_loop(1, rows - 1, inner_body, total)
    mean2 = total * (1.0 / count)

    def dev_body(r, acc):
        for c in range(0, width, CHUNK):
            v = row_chunk(r, c) - mean2
            acc = acc + jnp.sum((v * v).reshape(CHUNK // 8, 8, CP), axis=0)
        return acc

    devs2 = lax.fori_loop(0, rows, dev_body, jnp.zeros((8, CP), F32))
    stat2[0, 0:1, :] = mean2
    stat2[0, 1:2, :] = jnp.sum(devs2, axis=0, keepdims=True)
    stat2_copies = send_stats(stat2, s2s, s2r)
    for copy in w2_copies:
        copy.wait()
    for copy in stat2_copies:
        copy.wait_recv()
    m2, a2 = combine(stat2)

    def second_body(r, _):
        for c in range(0, width, CHUNK):
            act[pl.ds(8 + c, CHUNK), :] = silu_half((row_chunk(r, c) - m2) * a2)
        spread_row(r + 1)
        return 0

    lax.fori_loop(0, rows, second_body, 0)

    def out_copy(r):
        return pltpu.make_async_copy(outbuf.at[r], out_ref.at[0, r], out_sem.at[r])

    def final_row(r):
        outbuf[r] = (lat[1 + r].astype(F32) + conv(r, w2, 0, C)).astype(BF16)

    def final_inner(r, _):
        final_row(r)
        out_copy(r).start()
        return 0

    lax.fori_loop(1, rows - 1, final_inner, 0)

    def halo_row(k, r):
        off = murecv[k][0:1] - m2
        for c in range(0, width, CHUNK):
            v = hrecv[k, pl.ds(c, CHUNK), :].astype(F32)
            act[pl.ds(8 + c, CHUNK), :] = silu_half((v + off) * a2)
        spread_row(r)

    @pl.when(me > 0)
    def _():
        for copy in halo_copies(1):
            copy.wait_recv()
        halo_row(0, 0)

    @pl.when(me < B - 1)
    def _():
        for copy in halo_copies(0):
            copy.wait_recv()
        halo_row(1, rows + 1)

    def final_edge(k, _):
        r = k * (rows - 1)
        final_row(r)
        out_copy(r).start()
        return 0

    lax.fori_loop(0, 2, final_edge, 0)

    for copy in stat1_copies + slot_copies + p1_copies + p2_copies + p3_copies + stat2_copies:
        copy.wait_send()

    @pl.when(me > 0)
    def _():
        up_copy().wait_send()
        for copy in halo_copies(0):
            copy.wait_send()

    @pl.when(me < B - 1)
    def _():
        down_copy().wait_send()
        for copy in halo_copies(1):
            copy.wait_send()

    for r in range(rows):
        out_copy(r).wait()


def block(mesh_shape, lat, temb, ra, stored_row, w1, down, up, w2, tp):
    B, R = mesh_shape["band"], mesh_shape["req"]
    _, rows, width, C = lat.shape
    rank = up.shape[1]
    CP = round_up(C, LANES)
    piece = round_up(-(-(9 * C // 2 + 3 * rank) // B), 16)
    dims = (B, R, rows, width, C, rank, piece)
    ids = np.arange(CP) // (C // G)
    ok = np.arange(CP) < C
    gg = jnp.asarray((ids[:, None] == ids[None, :]) & ok[:, None] & ok[None, :], dtype=BF16)
    hbm = pl.BlockSpec(memory_space=pl.ANY)
    vmem = pl.BlockSpec(memory_space=pltpu.VMEM)
    smem = pl.BlockSpec(memory_space=pltpu.SMEM)
    V = pltpu.VMEM
    dma = lambda n: pltpu.SemaphoreType.DMA((n,))
    scratch = [
        V((rows + 2, width, C), BF16), V((width + 16, CP), F32), V((rows + 2, width, 1024), BF16),
        V((rows, width, CP), F32), V((3, 1024, C), BF16), V((3, 1024, C), BF16), V((3, 1024, LANES), BF16),
        V((64 + rank, CP), BF16), V(tp.shape, BF16), V(down.shape[1:], BF16), V(up.shape[1:], BF16), V((8, CP), F32),
        V((B, 8, CP), F32), V((B, 8, CP), F32), V((R, 8, LANES), jnp.int32), V((B * piece, LANES), BF16),
        V((B, piece, LANES), BF16), V((R, piece, LANES), BF16), V((R, piece, LANES), BF16), V((B, piece, LANES), BF16),
        V((2, width, CP), BF16), V((2, width, CP), BF16), V((2, 8, CP), F32), V((2, 8, CP), F32), V((rows, width, C), BF16),
        dma(4), dma(18), dma(18), dma(rows),
        dma(B), dma(B), dma(B), dma(B), dma(R), dma(R), dma(B), dma(B), dma(R), dma(R), dma(B), dma(B),
        dma(2), dma(2), dma(2), dma(2), dma(2), dma(2),
    ]
    return pl.pallas_call(
        functools.partial(kernel, dims),
        out_shape=jax.ShapeDtypeStruct(lat.shape, BF16),
        in_specs=[hbm, vmem, smem, smem, hbm, hbm, hbm, hbm, hbm, vmem],
        out_specs=hbm,
        scratch_shapes=scratch,
        compiler_params=pltpu.CompilerParams(
            collective_id=0, has_side_effects=True, vmem_limit_bytes=48 * 1024 * 1024),
        name="block",
    )(lat, temb, ra, stored_row, w1, down, up, w2, tp, gg)


def solution(mesh):
    in_specs = (
        P("req", "band", None, None),
        P("req", None),
        P("req", None),
        P(),
        P(),
        P(("band", "req"), None, None, None, None),
        P(("band", "req"), None, None),
        P(),
        P(),
    )
    return jax.shard_map(
        functools.partial(block, dict(mesh.shape)), mesh=mesh, in_specs=in_specs,
        out_specs=P("req", "band", None, None), check_vma=False)
```

```python
import functools

import jax
import jax.numpy as jnp
import numpy as np
from jax import lax
from jax.experimental import pallas as pl
from jax.experimental.pallas import tpu as pltpu
from jax.sharding import PartitionSpec as P

G = 32
EPS = 1e-05
MESH = pl.DeviceIdType.MESH
F32 = jnp.float32
BF16 = jnp.bfloat16
LANES = 128
CHUNK = 64


def round_up(value, step):
    return -(-value // step) * step


def split3(v):
    hi = v.astype(BF16)
    rest = v - hi.astype(F32)
    mid = rest.astype(BF16)
    return hi, mid, (rest - mid.astype(F32)).astype(BF16)


def kernel(
    dims,
    lat_ref, temb_ref, ra_ref, row_ref, w1_hbm, down_hbm, up_hbm, w2_hbm, tp_hbm, gg_ref,
    out_ref,
    lat, act, x, hid, w1, w2, rhs2, up_pad, tp, down, up, shift,
    stat1, stat2, slots, packed, recv1, sel, recv2, full,
    hsend, hrecv, musend, murecv, outbuf,
    ld_sem, w1_sem, w2_sem, out_sem,
    s1s, s1r, s2s, s2r, sls, slr, p1s, p1r, p2s, p2r, p3s, p3r, has, har, hbs, hbr, hms, hmr,
):
    B, R, rows, width, C, rank, piece = dims
    CP = round_up(C, LANES)
    count = rows * width
    me = lax.axis_index("band")
    mr = lax.axis_index("req")
    half = 9 * C // 2

    def band(d):
        return lax.rem(me + d, B)

    def req(e):
        return lax.rem(mr + e, R)

    ld = [
        pltpu.make_async_copy(lat_ref.at[0], lat.at[pl.ds(1, rows)], ld_sem.at[0]),
        pltpu.make_async_copy(down_hbm.at[0], down, ld_sem.at[1]),
        pltpu.make_async_copy(up_hbm.at[0], up, ld_sem.at[2]),
        pltpu.make_async_copy(tp_hbm, tp, ld_sem.at[3]),
    ]
    for copy in ld:
        copy.start()

    def weight_copies(src, dst, sems):
        copies = []
        for i in range(3):
            for j in range(3):
                k = (i * 3 + j) * 2
                copies.append(pltpu.make_async_copy(
                    src.at[i, j, pl.ds(0, 256)], dst.at[i, pl.ds(256 * j, 256)], sems.at[k]))
                copies.append(pltpu.make_async_copy(
                    src.at[i, j, pl.ds(256, 64)], dst.at[i, pl.ds(768 + 64 * j, 64)], sems.at[k + 1]))
        return copies

    w1_copies = weight_copies(w1_hbm, w1, w1_sem)
    w2_copies = weight_copies(w2_hbm, w2, w2_sem)
    for copy in w1_copies + w2_copies:
        copy.start()

    barrier = pltpu.get_barrier_semaphore()
    for d in range(1, B):
        pl.semaphore_signal(barrier, inc=1, device_id={"band": band(d)}, device_id_type=MESH)
    for e in range(1, R):
        pl.semaphore_signal(barrier, inc=1, device_id={"req": req(e)}, device_id_type=MESH)

    slot = row_ref[ra_ref[0, 0]]
    slots[0] = jnp.full((8, LANES), slot, jnp.int32)
    ld[1].wait()
    ld[2].wait()
    flat = packed
    total_rows = half + 3 * rank
    zero64 = jnp.zeros((rank, 64), BF16)
    tap = [down[t // 3, t % 3].astype(F32).T.astype(BF16) for t in range(9)]
    for start in range(0, half, 160):
        t0, c0 = start // C, start % C
        t1, c1 = (start + half) // C, (start + half) % C
        flat[pl.ds(start, 160), :] = jnp.concatenate([tap[t0][c0:c0 + 160], tap[t1][c1:c1 + 160]], axis=1)
    flat[pl.ds(half, rank), :] = up[:, 0:128]
    flat[pl.ds(half + rank, rank), :] = up[:, 128:256]
    flat[pl.ds(half + 2 * rank, rank), :] = jnp.concatenate([up[:, 256:320], zero64], axis=1)
    pad_rows = B * piece - total_rows
    if pad_rows:
        flat[pl.ds(total_rows, pad_rows), :] = jnp.zeros((pad_rows, LANES), BF16)

    ld[0].wait()
    shift[...] = jnp.zeros_like(shift)
    stat1[0] = jnp.zeros((8, CP), F32)
    stat2[0] = jnp.zeros((8, CP), F32)

    def lat_sum(k, acc):
        v = lat[1 + k // (width // CHUNK), pl.ds(pl.multiple_of((k % (width // CHUNK)) * CHUNK, CHUNK), CHUNK), :].astype(F32)
        return acc + jnp.sum(v.reshape(CHUNK // 8, 8, C), axis=0)

    steps = rows * (width // CHUNK)
    sums = lax.fori_loop(0, steps, lat_sum, jnp.zeros((8, C), F32))
    mean = jnp.sum(sums, axis=0, keepdims=True) * (1.0 / count)

    def lat_dev(k, acc):
        v = lat[1 + k // (width // CHUNK), pl.ds(pl.multiple_of((k % (width // CHUNK)) * CHUNK, CHUNK), CHUNK), :].astype(F32)
        v = v - mean
        return acc + jnp.sum((v * v).reshape(CHUNK // 8, 8, C), axis=0)

    devs = lax.fori_loop(0, steps, lat_dev, jnp.zeros((8, C), F32))
    stat1[0, 0:1, 0:C] = mean
    stat1[0, 1:2, 0:C] = jnp.sum(devs, axis=0, keepdims=True)

    pl.semaphore_wait(barrier, B - 1 + R - 1)

    def send_stats(buf, ss, rs):
        out = []
        for d in range(1, B):
            out.append(pltpu.make_async_remote_copy(
                src_ref=buf.at[0], dst_ref=buf.at[d], send_sem=ss.at[d], recv_sem=rs.at[d],
                device_id={"band": band(d)}, device_id_type=MESH))
            out[-1].start()
        return out

    stat1_copies = send_stats(stat1, s1s, s1r)
    slot_copies = []
    for e in range(1, R):
        slot_copies.append(pltpu.make_async_remote_copy(
            src_ref=slots.at[0], dst_ref=slots.at[e], send_sem=sls.at[e], recv_sem=slr.at[e],
            device_id={"req": req(e)}, device_id_type=MESH))
        slot_copies[-1].start()

    def up_copy():
        return pltpu.make_async_remote_copy(
            src_ref=lat.at[1], dst_ref=lat.at[rows + 1], send_sem=has.at[0], recv_sem=har.at[0],
            device_id={"band": lax.rem(me + B - 1, B)}, device_id_type=MESH)

    def down_copy():
        return pltpu.make_async_remote_copy(
            src_ref=lat.at[rows], dst_ref=lat.at[0], send_sem=has.at[1], recv_sem=har.at[1],
            device_id={"band": band(1)}, device_id_type=MESH)

    @pl.when(me > 0)
    def _():
        up_copy().start()

    @pl.when(me < B - 1)
    def _():
        down_copy().start()

    p1_copies = []
    for d in range(1, B):
        p1_copies.append(pltpu.make_async_remote_copy(
            src_ref=packed.at[pl.ds(pl.multiple_of(band(d) * piece, 16), piece)], dst_ref=recv1.at[d],
            send_sem=p1s.at[d], recv_sem=p1r.at[d], device_id={"band": band(d)}, device_id_type=MESH))
        p1_copies[-1].start()

    ld[3].wait()
    t = temb_ref[...].astype(F32)
    t = (t / (1.0 + jnp.exp(-t))).astype(BF16).astype(F32)
    t = jnp.broadcast_to(t, (16, t.shape[1])).astype(BF16)
    shift[0:1, 0:C] = lax.dot_general(
        t, tp[...], (((1,), (1,)), ((), ())), preferred_element_type=F32)[0:1]

    act[...] = jnp.zeros_like(act)
    for i in range(3):
        w1[i, pl.ds(960, 64), :] = jnp.zeros((64, C), BF16)
        w2[i, pl.ds(960, 64), :] = jnp.zeros((64, C), BF16)
        rhs2[i, pl.ds(960, 64), :] = jnp.zeros((64, LANES), BF16)

    def group_sum(v):
        v = jnp.broadcast_to(v, (16, CP))
        gg = gg_ref[...]
        return sum(jnp.dot(part, gg, preferred_element_type=F32) for part in split3(v))[0:1]

    def combine(buf):
        cpg = C // G
        total = buf[0]
        for d in range(1, B):
            total = total + buf[d]
        m = group_sum(total[0:1]) * (1.0 / (cpg * B))
        dev = jnp.zeros((1, CP), F32)
        for d in range(B):
            diff = buf[d][0:1] - m
            dev = dev + diff * diff
        valid = lax.broadcasted_iota(jnp.int32, (1, CP), 1) < C
        dev = jnp.where(valid, total[1:2] + float(count) * dev, 0.0)
        spread = group_sum(dev) * (1.0 / (float(count) * cpg * B))
        return m, 0.5 * lax.rsqrt(spread + EPS)

    def silu_half(h):
        return h * jnp.tanh(h) + h

    def spread_row(r):
        for c in range(0, width, CHUNK):
            v = act[pl.ds(c, CHUNK + 16), :]
            before = pltpu.roll(v, 1, 0)[8:8 + CHUNK]
            after = pltpu.roll(v, CHUNK + 15, 0)[8:8 + CHUNK]
            here = v[8:8 + CHUNK]
            x[r, pl.ds(c, CHUNK), 0:256] = before[:, 0:256].astype(BF16)
            x[r, pl.ds(c, CHUNK), 256:512] = here[:, 0:256].astype(BF16)
            x[r, pl.ds(c, CHUNK), 512:768] = after[:, 0:256].astype(BF16)
            x[r, pl.ds(c, CHUNK), 768:896] = (before[:, 256:384] + pltpu.roll(here[:, 256:384], 64, 1)).astype(BF16)
            x[r, pl.ds(c, CHUNK), 896:1024] = after[:, 256:384].astype(BF16)

    for copy in stat1_copies:
        copy.wait_recv()
    m1, a1 = combine(stat1)
    m1, a1 = m1[:, 0:C], a1[:, 0:C]

    def first_row(r):
        for c in range(0, width, CHUNK):
            v = lat[r, pl.ds(c, CHUNK), :].astype(F32)
            act[pl.ds(8 + c, CHUNK), 0:C] = silu_half((v - m1) * a1)
        spread_row(r)

    def first_body(k, _):
        first_row(1 + k)
        return 0

    lax.fori_loop(0, rows, first_body, 0)

    for copy in p1_copies + slot_copies:
        copy.wait_recv()
    p2_copies = []
    own = packed[pl.ds(pl.multiple_of(me * piece, 16), piece), :].astype(F32)
    for n in range(R):
        e = (n + 1) % R
        wanted = slots[(R - e) % R][0:1]
        acc = own * (wanted == me * R + mr).astype(F32)
        for d in range(1, B):
            ident = lax.rem(me - d + B, B) * R + mr
            acc = acc + recv1[d].astype(F32) * (wanted == ident).astype(F32)
        sel[e] = acc.astype(BF16)
        if e:
            p2_copies.append(pltpu.make_async_remote_copy(
                src_ref=sel.at[e], dst_ref=recv2.at[e], send_sem=p2s.at[e], recv_sem=p2r.at[e],
                device_id={"req": req(e)}, device_id_type=MESH))
            p2_copies[-1].start()

    for copy in w1_copies:
        copy.wait()

    def conv(r, weights, lo, hi):
        total = None
        for i in range(3):
            term = jnp.dot(x[r + i], weights[i, :, lo:hi], preferred_element_type=F32)
            total = term if total is None else total + term
        return total

    def main_body(r, _):
        hid[r, :, 0:256] = conv(r, w1, 0, 256) + shift[0:1, 0:256]
        return 0

    lax.fori_loop(1, rows - 1, main_body, 0)

    for copy in p2_copies:
        copy.wait_recv()
    acc = sel[0].astype(F32)
    for e in range(1, R):
        acc = acc + recv2[e].astype(F32)
    full[me] = acc.astype(BF16)
    p3_copies = []
    for d in range(1, B):
        p3_copies.append(pltpu.make_async_remote_copy(
            src_ref=full.at[me], dst_ref=full.at[me], send_sem=p3s.at[d], recv_sem=p3r.at[d],
            device_id={"band": band(d)}, device_id_type=MESH))
        p3_copies[-1].start()

    zero_row = jnp.zeros((width, 1024), BF16)

    @pl.when(me > 0)
    def _():
        down_copy().wait_recv()
        first_row(0)

    @pl.when(me == 0)
    def _():
        x[0] = zero_row

    @pl.when(me < B - 1)
    def _():
        up_copy().wait_recv()
        first_row(rows + 1)

    @pl.when(me == B - 1)
    def _():
        x[rows + 1] = zero_row

    lax.fori_loop(0, 2, lambda k, c: main_body(k * (rows - 1), c), 0)

    for d in range(1, B):
        pltpu.make_async_remote_copy(
            src_ref=full.at[me], dst_ref=full.at[lax.rem(me - d + B, B)], send_sem=p3s.at[d], recv_sem=p3r.at[d],
            device_id={"band": band(d)}, device_id_type=MESH).wait_recv()

    low_lane = lax.broadcasted_iota(jnp.int32, (1, LANES), 1) < 64

    def adapter_rows(start, size):
        parts = []
        while size:
            p, o = start // piece, start % piece
            take = min(size, piece - o)
            parts.append(full[p, pl.ds(o, take), :].astype(F32))
            start, size = start + take, size - take
        return parts[0] if len(parts) == 1 else jnp.concatenate(parts, axis=0)

    def place(i, k, start, size):
        main3 = w1[i, pl.ds(k, size), 256:320].astype(F32)
        main3 = jnp.concatenate([main3, jnp.zeros((size, 64), F32)], axis=1)
        if start < half:
            v = pltpu.roll(adapter_rows(start, size), 64, 1)
        else:
            v = adapter_rows(start - half, size)
        rhs2[i, pl.ds(k, size), :] = jnp.where(low_lane, main3, v).astype(BF16)

    for i in range(3):
        for j in range(3):
            base = (i * 3 + j) * C
            for c in range(0, C, 32):
                k = 256 * j + c if c < 256 else 768 + 64 * j + c - 256
                place(i, k, base + c, 32)
    up_pad[pl.ds(0, 64), :] = jnp.zeros((64, CP), BF16)
    for b in range(3):
        up_pad[pl.ds(64, rank), 128 * b:128 * b + 128] = adapter_rows(half + b * rank, rank).astype(BF16)

    def hidden_row(r):
        t = conv(r, rhs2, 0, 128)
        lifted = jnp.dot(t.astype(BF16), up_pad[...], preferred_element_type=F32)
        hid[r, :, 0:256] = hid[r, :, 0:256] + lifted[:, 0:256]
        hid[r, :, 256:384] = jnp.where(low_lane, t, 0.0) + lifted[:, 256:384] + shift[0:1, 256:384]

    def row_chunk(r, c):
        return hid[r, pl.ds(c, CHUNK), :]

    def row_sum(r):
        acc = jnp.zeros((8, CP), F32)
        for c in range(0, width, CHUNK):
            acc = acc + jnp.sum(row_chunk(r, c).reshape(CHUNK // 8, 8, CP), axis=0)
        return jnp.sum(acc, axis=0, keepdims=True)

    def edge_body(k, acc):
        r = k * (rows - 1)
        hidden_row(r)
        total = row_sum(r)
        mu = total * (1.0 / width)
        musend[k] = jnp.broadcast_to(mu, (8, CP))
        for c in range(0, width, CHUNK):
            hsend[k, pl.ds(c, CHUNK), :] = (row_chunk(r, c) - mu).astype(BF16)
        return acc + total

    def halo_copies(k):
        target = lax.rem(me + B - 1, B) if k == 0 else band(1)
        return (
            pltpu.make_async_remote_copy(
                src_ref=hsend.at[k], dst_ref=hrecv.at[1 - k], send_sem=hbs.at[k], recv_sem=hbr.at[k],
                device_id={"band": target}, device_id_type=MESH),
            pltpu.make_async_remote_copy(
                src_ref=musend.at[k], dst_ref=murecv.at[1 - k], send_sem=hms.at[k], recv_sem=hmr.at[k],
                device_id={"band": target}, device_id_type=MESH),
        )

    total = lax.fori_loop(0, 2, edge_body, jnp.zeros((1, CP), F32))

    @pl.when(me > 0)
    def _():
        for copy in halo_copies(0):
            copy.start()

    @pl.when(me < B - 1)
    def _():
        for copy in halo_copies(1):
            copy.start()

    def inner_body(r, acc):
        hidden_row(r)
        return acc + row_sum(r)

    total = lax.fori_loop(1, rows - 1, inner_body, total)
    mean2 = total * (1.0 / count)

    def dev_body(r, acc):
        for c in range(0, width, CHUNK):
            v = row_chunk(r, c) - mean2
            acc = acc + jnp.sum((v * v).reshape(CHUNK // 8, 8, CP), axis=0)
        return acc

    devs2 = lax.fori_loop(0, rows, dev_body, jnp.zeros((8, CP), F32))
    stat2[0, 0:1, :] = mean2
    stat2[0, 1:2, :] = jnp.sum(devs2, axis=0, keepdims=True)
    stat2_copies = send_stats(stat2, s2s, s2r)
    for copy in w2_copies:
        copy.wait()
    for copy in stat2_copies:
        copy.wait_recv()
    m2, a2 = combine(stat2)

    def second_body(r, _):
        for c in range(0, width, CHUNK):
            act[pl.ds(8 + c, CHUNK), :] = silu_half((row_chunk(r, c) - m2) * a2)
        spread_row(r + 1)
        return 0

    lax.fori_loop(0, rows, second_body, 0)

    def out_copy(r):
        return pltpu.make_async_copy(outbuf.at[r], out_ref.at[0, r], out_sem.at[r])

    def final_row(r):
        outbuf[r] = (lat[1 + r].astype(F32) + conv(r, w2, 0, C)).astype(BF16)

    def final_inner(r, _):
        final_row(r)
        out_copy(r).start()
        return 0

    lax.fori_loop(1, rows - 1, final_inner, 0)

    def halo_row(k, r):
        off = murecv[k][0:1] - m2
        for c in range(0, width, CHUNK):
            v = hrecv[k, pl.ds(c, CHUNK), :].astype(F32)
            act[pl.ds(8 + c, CHUNK), :] = silu_half((v + off) * a2)
        spread_row(r)

    @pl.when(me > 0)
    def _():
        for copy in halo_copies(1):
            copy.wait_recv()
        halo_row(0, 0)

    @pl.when(me < B - 1)
    def _():
        for copy in halo_copies(0):
            copy.wait_recv()
        halo_row(1, rows + 1)

    def final_edge(k, _):
        r = k * (rows - 1)
        final_row(r)
        out_copy(r).start()
        return 0

    lax.fori_loop(0, 2, final_edge, 0)

    for copy in stat1_copies + slot_copies + p1_copies + p2_copies + p3_copies + stat2_copies:
        copy.wait_send()

    @pl.when(me > 0)
    def _():
        up_copy().wait_send()
        for copy in halo_copies(0):
            copy.wait_send()

    @pl.when(me < B - 1)
    def _():
        down_copy().wait_send()
        for copy in halo_copies(1):
            copy.wait_send()

    for r in range(rows):
        out_copy(r).wait()


def block(mesh_shape, lat, temb, ra, stored_row, w1, down, up, w2, tp):
    B, R = mesh_shape["band"], mesh_shape["req"]
    _, rows, width, C = lat.shape
    rank = up.shape[1]
    down = jnp.swapaxes(down, 3, 4)
    tp = tp.T
    CP = round_up(C, LANES)
    piece = round_up(-(-(9 * C // 2 + 3 * rank) // B), 16)
    dims = (B, R, rows, width, C, rank, piece)
    ids = np.arange(CP) // (C // G)
    ok = np.arange(CP) < C
    gg = jnp.asarray((ids[:, None] == ids[None, :]) & ok[:, None] & ok[None, :], dtype=BF16)
    hbm = pl.BlockSpec(memory_space=pl.ANY)
    vmem = pl.BlockSpec(memory_space=pltpu.VMEM)
    smem = pl.BlockSpec(memory_space=pltpu.SMEM)
    V = pltpu.VMEM
    dma = lambda n: pltpu.SemaphoreType.DMA((n,))
    scratch = [
        V((rows + 2, width, C), BF16), V((width + 16, CP), F32), V((rows + 2, width, 1024), BF16),
        V((rows, width, CP), F32), V((3, 1024, C), BF16), V((3, 1024, C), BF16), V((3, 1024, LANES), BF16),
        V((64 + rank, CP), BF16), V(tp.shape, BF16), V(down.shape[1:], BF16), V(up.shape[1:], BF16), V((8, CP), F32),
        V((B, 8, CP), F32), V((B, 8, CP), F32), V((R, 8, LANES), jnp.int32), V((B * piece, LANES), BF16),
        V((B, piece, LANES), BF16), V((R, piece, LANES), BF16), V((R, piece, LANES), BF16), V((B, piece, LANES), BF16),
        V((2, width, CP), BF16), V((2, width, CP), BF16), V((2, 8, CP), F32), V((2, 8, CP), F32), V((rows, width, C), BF16),
        dma(4), dma(18), dma(18), dma(rows),
        dma(B), dma(B), dma(B), dma(B), dma(R), dma(R), dma(B), dma(B), dma(R), dma(R), dma(B), dma(B),
        dma(2), dma(2), dma(2), dma(2), dma(2), dma(2),
    ]
    return pl.pallas_call(
        functools.partial(kernel, dims),
        out_shape=jax.ShapeDtypeStruct(lat.shape, BF16),
        in_specs=[hbm, vmem, smem, smem, hbm, hbm, hbm, hbm, hbm, vmem],
        out_specs=hbm,
        scratch_shapes=scratch,
        compiler_params=pltpu.CompilerParams(
            collective_id=0, has_side_effects=True, vmem_limit_bytes=48 * 1024 * 1024),
        name="block",
    )(lat, temb, ra, stored_row, w1, down, up, w2, tp, gg)


def solution(mesh):
    in_specs = (
        P("req", "band", None, None),
        P("req", None),
        P("req", None),
        P(),
        P(),
        P(("band", "req"), None, None, None, None),
        P(("band", "req"), None, None),
        P(),
        P(),
    )
    return jax.shard_map(
        functools.partial(block, dict(mesh.shape)), mesh=mesh, in_specs=in_specs,
        out_specs=P("req", "band", None, None), check_vma=False)
```

```python
import functools

import jax
import jax.numpy as jnp
import numpy as np
from jax import lax
from jax.experimental import pallas as pl
from jax.experimental.pallas import tpu as pltpu
from jax.sharding import PartitionSpec as P

G = 32
EPS = 1e-05
MESH = pl.DeviceIdType.MESH
F32 = jnp.float32
BF16 = jnp.bfloat16
LANES = 128
CHUNK = 64


def round_up(value, step):
    return -(-value // step) * step


def split3(v):
    hi = v.astype(BF16)
    rest = v - hi.astype(F32)
    mid = rest.astype(BF16)
    return hi, mid, (rest - mid.astype(F32)).astype(BF16)


def kernel(
    dims,
    lat_ref, temb_ref, ra_ref, row_ref, w1_hbm, down_hbm, up_hbm, w2_hbm, tp_hbm, gg_ref,
    out_ref,
    lat, act, x, hid, w1, w2, rhs2, up_pad, tp, down, up, shift,
    stat1, stat2, slots, packed, recv1, sel, recv2, full,
    hsend, hrecv, musend, murecv, outbuf,
    ld_sem, w1_sem, w2_sem, out_sem,
    s1s, s1r, s2s, s2r, sls, slr, p1s, p1r, p2s, p2r, p3s, p3r, has, har, hbs, hbr, hms, hmr,
):
    B, R, rows, width, C, rank, piece = dims
    CP = round_up(C, LANES)
    count = rows * width
    me = lax.axis_index("band")
    mr = lax.axis_index("req")
    half = 9 * C // 2

    def band(d):
        return lax.rem(me + d, B)

    def req(e):
        return lax.rem(mr + e, R)

    ld = [
        pltpu.make_async_copy(lat_ref.at[0], lat.at[pl.ds(1, rows)], ld_sem.at[0]),
        pltpu.make_async_copy(down_hbm.at[0], down, ld_sem.at[1]),
        pltpu.make_async_copy(up_hbm.at[0], up, ld_sem.at[2]),
        pltpu.make_async_copy(tp_hbm, tp, ld_sem.at[3]),
    ]
    for copy in ld:
        copy.start()

    def weight_copies(src, dst, sems):
        copies = []
        for i in range(3):
            for j in range(3):
                k = (i * 3 + j) * 2
                copies.append(pltpu.make_async_copy(
                    src.at[i, j, pl.ds(0, 256)], dst.at[i, pl.ds(256 * j, 256)], sems.at[k]))
                copies.append(pltpu.make_async_copy(
                    src.at[i, j, pl.ds(256, 64)], dst.at[i, pl.ds(768 + 64 * j, 64)], sems.at[k + 1]))
        return copies

    w1_copies = weight_copies(w1_hbm, w1, w1_sem)
    w2_copies = weight_copies(w2_hbm, w2, w2_sem)
    for copy in w1_copies + w2_copies:
        copy.start()

    barrier = pltpu.get_barrier_semaphore()
    for d in range(1, B):
        pl.semaphore_signal(barrier, inc=1, device_id={"band": band(d)}, device_id_type=MESH)
    for e in range(1, R):
        pl.semaphore_signal(barrier, inc=1, device_id={"req": req(e)}, device_id_type=MESH)

    slot = row_ref[ra_ref[0, 0]]
    slots[0] = jnp.full((8, LANES), slot, jnp.int32)
    ld[1].wait()
    ld[2].wait()
    flat = packed
    total_rows = half + 3 * rank
    zero64 = jnp.zeros((rank, 64), BF16)
    for start in range(0, half, 160):
        t0, c0 = start // C, start % C
        t1, c1 = (start + half) // C, (start + half) % C
        flat[pl.ds(start, 160), :] = jnp.concatenate(
            [down[t0 // 3, t0 % 3, pl.ds(c0, 160), :], down[t1 // 3, t1 % 3, pl.ds(c1, 160), :]], axis=1)
    flat[pl.ds(half, rank), :] = up[:, 0:128]
    flat[pl.ds(half + rank, rank), :] = up[:, 128:256]
    flat[pl.ds(half + 2 * rank, rank), :] = jnp.concatenate([up[:, 256:320], zero64], axis=1)
    pad_rows = B * piece - total_rows
    if pad_rows:
        flat[pl.ds(total_rows, pad_rows), :] = jnp.zeros((pad_rows, LANES), BF16)

    ld[0].wait()
    shift[...] = jnp.zeros_like(shift)
    stat1[0] = jnp.zeros((8, CP), F32)
    stat2[0] = jnp.zeros((8, CP), F32)

    def lat_sum(k, acc):
        v = lat[1 + k // (width // CHUNK), pl.ds(pl.multiple_of((k % (width // CHUNK)) * CHUNK, CHUNK), CHUNK), :].astype(F32)
        return acc + jnp.sum(v.reshape(CHUNK // 8, 8, C), axis=0)

    steps = rows * (width // CHUNK)
    sums = lax.fori_loop(0, steps, lat_sum, jnp.zeros((8, C), F32))
    mean = jnp.sum(sums, axis=0, keepdims=True) * (1.0 / count)

    def lat_dev(k, acc):
        v = lat[1 + k // (width // CHUNK), pl.ds(pl.multiple_of((k % (width // CHUNK)) * CHUNK, CHUNK), CHUNK), :].astype(F32)
        v = v - mean
        return acc + jnp.sum((v * v).reshape(CHUNK // 8, 8, C), axis=0)

    devs = lax.fori_loop(0, steps, lat_dev, jnp.zeros((8, C), F32))
    stat1[0, 0:1, 0:C] = mean
    stat1[0, 1:2, 0:C] = jnp.sum(devs, axis=0, keepdims=True)

    pl.semaphore_wait(barrier, B - 1 + R - 1)

    def send_stats(buf, ss, rs):
        out = []
        for d in range(1, B):
            out.append(pltpu.make_async_remote_copy(
                src_ref=buf.at[0], dst_ref=buf.at[d], send_sem=ss.at[d], recv_sem=rs.at[d],
                device_id={"band": band(d)}, device_id_type=MESH))
            out[-1].start()
        return out

    stat1_copies = send_stats(stat1, s1s, s1r)
    slot_copies = []
    for e in range(1, R):
        slot_copies.append(pltpu.make_async_remote_copy(
            src_ref=slots.at[0], dst_ref=slots.at[e], send_sem=sls.at[e], recv_sem=slr.at[e],
            device_id={"req": req(e)}, device_id_type=MESH))
        slot_copies[-1].start()

    p1_copies = []
    for d in range(1, B):
        p1_copies.append(pltpu.make_async_remote_copy(
            src_ref=packed.at[pl.ds(pl.multiple_of(band(d) * piece, 16), piece)], dst_ref=recv1.at[d],
            send_sem=p1s.at[d], recv_sem=p1r.at[d], device_id={"band": band(d)}, device_id_type=MESH))
        p1_copies[-1].start()

    def up_copy():
        return pltpu.make_async_remote_copy(
            src_ref=lat.at[1], dst_ref=lat.at[rows + 1], send_sem=has.at[0], recv_sem=har.at[0],
            device_id={"band": lax.rem(me + B - 1, B)}, device_id_type=MESH)

    def down_copy():
        return pltpu.make_async_remote_copy(
            src_ref=lat.at[rows], dst_ref=lat.at[0], send_sem=has.at[1], recv_sem=har.at[1],
            device_id={"band": band(1)}, device_id_type=MESH)

    @pl.when(me > 0)
    def _():
        up_copy().start()

    @pl.when(me < B - 1)
    def _():
        down_copy().start()

    ld[3].wait()
    t = temb_ref[...].astype(F32)
    t = (t / (1.0 + jnp.exp(-t))).astype(BF16).astype(F32)
    t = jnp.broadcast_to(t, (16, t.shape[1])).astype(BF16)
    shift[0:1, 0:C] = lax.dot_general(
        t, tp[...], (((1,), (1,)), ((), ())), preferred_element_type=F32)[0:1]

    act[...] = jnp.zeros_like(act)
    for i in range(3):
        w1[i, pl.ds(960, 64), :] = jnp.zeros((64, C), BF16)
        w2[i, pl.ds(960, 64), :] = jnp.zeros((64, C), BF16)
        rhs2[i, pl.ds(960, 64), :] = jnp.zeros((64, LANES), BF16)

    def group_sum(v):
        v = jnp.broadcast_to(v, (16, CP))
        gg = gg_ref[...]
        return sum(jnp.dot(part, gg, preferred_element_type=F32) for part in split3(v))[0:1]

    def combine(buf):
        cpg = C // G
        total = buf[0]
        for d in range(1, B):
            total = total + buf[d]
        m = group_sum(total[0:1]) * (1.0 / (cpg * B))
        dev = jnp.zeros((1, CP), F32)
        for d in range(B):
            diff = buf[d][0:1] - m
            dev = dev + diff * diff
        valid = lax.broadcasted_iota(jnp.int32, (1, CP), 1) < C
        dev = jnp.where(valid, total[1:2] + float(count) * dev, 0.0)
        spread = group_sum(dev) * (1.0 / (float(count) * cpg * B))
        return m, 0.5 * lax.rsqrt(spread + EPS)

    def silu_half(h):
        return h * jnp.tanh(h) + h

    def spread_row(r):
        for c in range(0, width, CHUNK):
            v = act[pl.ds(c, CHUNK + 16), :]
            before = pltpu.roll(v, 1, 0)[8:8 + CHUNK]
            after = pltpu.roll(v, CHUNK + 15, 0)[8:8 + CHUNK]
            here = v[8:8 + CHUNK]
            x[r, pl.ds(c, CHUNK), 0:256] = before[:, 0:256].astype(BF16)
            x[r, pl.ds(c, CHUNK), 256:512] = here[:, 0:256].astype(BF16)
            x[r, pl.ds(c, CHUNK), 512:768] = after[:, 0:256].astype(BF16)
            x[r, pl.ds(c, CHUNK), 768:896] = (before[:, 256:384] + pltpu.roll(here[:, 256:384], 64, 1)).astype(BF16)
            x[r, pl.ds(c, CHUNK), 896:1024] = after[:, 256:384].astype(BF16)

    for copy in stat1_copies:
        copy.wait_recv()
    m1, a1 = combine(stat1)
    m1, a1 = m1[:, 0:C], a1[:, 0:C]

    def first_row(r):
        for c in range(0, width, CHUNK):
            v = lat[r, pl.ds(c, CHUNK), :].astype(F32)
            act[pl.ds(8 + c, CHUNK), 0:C] = silu_half((v - m1) * a1)
        spread_row(r)

    def first_body(k, _):
        first_row(1 + k)
        return 0

    lax.fori_loop(0, rows, first_body, 0)

    for copy in p1_copies + slot_copies:
        copy.wait_recv()
    p2_copies = []
    own = packed[pl.ds(pl.multiple_of(me * piece, 16), piece), :].astype(F32)
    for n in range(R):
        e = (n + 1) % R
        wanted = slots[(R - e) % R][0:1]
        acc = own * (wanted == me * R + mr).astype(F32)
        for d in range(1, B):
            ident = lax.rem(me - d + B, B) * R + mr
            acc = acc + recv1[d].astype(F32) * (wanted == ident).astype(F32)
        sel[e] = acc.astype(BF16)
        if e:
            p2_copies.append(pltpu.make_async_remote_copy(
                src_ref=sel.at[e], dst_ref=recv2.at[e], send_sem=p2s.at[e], recv_sem=p2r.at[e],
                device_id={"req": req(e)}, device_id_type=MESH))
            p2_copies[-1].start()

    for copy in w1_copies:
        copy.wait()

    def conv(r, weights, lo, hi):
        total = None
        for i in range(3):
            term = jnp.dot(x[r + i], weights[i, :, lo:hi], preferred_element_type=F32)
            total = term if total is None else total + term
        return total

    def main_body(r, _):
        hid[r, :, 0:256] = conv(r, w1, 0, 256) + shift[0:1, 0:256]
        return 0

    lax.fori_loop(1, rows - 1, main_body, 0)

    for copy in p2_copies:
        copy.wait_recv()
    acc = sel[0].astype(F32)
    for e in range(1, R):
        acc = acc + recv2[e].astype(F32)
    full[me] = acc.astype(BF16)
    p3_copies = []
    for d in range(1, B):
        p3_copies.append(pltpu.make_async_remote_copy(
            src_ref=full.at[me], dst_ref=full.at[me], send_sem=p3s.at[d], recv_sem=p3r.at[d],
            device_id={"band": band(d)}, device_id_type=MESH))
        p3_copies[-1].start()

    zero_row = jnp.zeros((width, 1024), BF16)

    @pl.when(me > 0)
    def _():
        down_copy().wait_recv()
        first_row(0)

    @pl.when(me == 0)
    def _():
        x[0] = zero_row

    @pl.when(me < B - 1)
    def _():
        up_copy().wait_recv()
        first_row(rows + 1)

    @pl.when(me == B - 1)
    def _():
        x[rows + 1] = zero_row

    lax.fori_loop(0, 2, lambda k, c: main_body(k * (rows - 1), c), 0)

    for d in range(1, B):
        pltpu.make_async_remote_copy(
            src_ref=full.at[me], dst_ref=full.at[lax.rem(me - d + B, B)], send_sem=p3s.at[d], recv_sem=p3r.at[d],
            device_id={"band": band(d)}, device_id_type=MESH).wait_recv()

    low_lane = lax.broadcasted_iota(jnp.int32, (1, LANES), 1) < 64

    def adapter_rows(start, size):
        parts = []
        while size:
            p, o = start // piece, start % piece
            take = min(size, piece - o)
            parts.append(full[p, pl.ds(o, take), :].astype(F32))
            start, size = start + take, size - take
        return parts[0] if len(parts) == 1 else jnp.concatenate(parts, axis=0)

    def place(i, k, start, size):
        main3 = w1[i, pl.ds(k, size), 256:320].astype(F32)
        main3 = jnp.concatenate([main3, jnp.zeros((size, 64), F32)], axis=1)
        if start < half:
            v = pltpu.roll(adapter_rows(start, size), 64, 1)
        else:
            v = adapter_rows(start - half, size)
        rhs2[i, pl.ds(k, size), :] = jnp.where(low_lane, main3, v).astype(BF16)

    for i in range(3):
        for j in range(3):
            base = (i * 3 + j) * C
            for c in range(0, C, 32):
                k = 256 * j + c if c < 256 else 768 + 64 * j + c - 256
                place(i, k, base + c, 32)
    up_pad[pl.ds(0, 64), :] = jnp.zeros((64, CP), BF16)
    for b in range(3):
        up_pad[pl.ds(64, rank), 128 * b:128 * b + 128] = adapter_rows(half + b * rank, rank).astype(BF16)

    def hidden_row(r):
        t = conv(r, rhs2, 0, 128)
        lifted = jnp.dot(t.astype(BF16), up_pad[...], preferred_element_type=F32)
        hid[r, :, 0:256] = hid[r, :, 0:256] + lifted[:, 0:256]
        hid[r, :, 256:384] = jnp.where(low_lane, t, 0.0) + lifted[:, 256:384] + shift[0:1, 256:384]

    def row_chunk(r, c):
        return hid[r, pl.ds(c, CHUNK), :]

    def row_sum(r):
        acc = jnp.zeros((8, CP), F32)
        for c in range(0, width, CHUNK):
            acc = acc + jnp.sum(row_chunk(r, c).reshape(CHUNK // 8, 8, CP), axis=0)
        return jnp.sum(acc, axis=0, keepdims=True)

    def edge_body(k, acc):
        r = k * (rows - 1)
        hidden_row(r)
        total = row_sum(r)
        mu = total * (1.0 / width)
        musend[k] = jnp.broadcast_to(mu, (8, CP))
        for c in range(0, width, CHUNK):
            hsend[k, pl.ds(c, CHUNK), :] = (row_chunk(r, c) - mu).astype(BF16)
        return acc + total

    def halo_copies(k):
        target = lax.rem(me + B - 1, B) if k == 0 else band(1)
        return (
            pltpu.make_async_remote_copy(
                src_ref=hsend.at[k], dst_ref=hrecv.at[1 - k], send_sem=hbs.at[k], recv_sem=hbr.at[k],
                device_id={"band": target}, device_id_type=MESH),
            pltpu.make_async_remote_copy(
                src_ref=musend.at[k], dst_ref=murecv.at[1 - k], send_sem=hms.at[k], recv_sem=hmr.at[k],
                device_id={"band": target}, device_id_type=MESH),
        )

    total = lax.fori_loop(0, 2, edge_body, jnp.zeros((1, CP), F32))

    @pl.when(me > 0)
    def _():
        for copy in halo_copies(0):
            copy.start()

    @pl.when(me < B - 1)
    def _():
        for copy in halo_copies(1):
            copy.start()

    def inner_body(r, acc):
        hidden_row(r)
        return acc + row_sum(r)

    total = lax.fori_loop(1, rows - 1, inner_body, total)
    mean2 = total * (1.0 / count)

    def dev_body(r, acc):
        for c in range(0, width, CHUNK):
            v = row_chunk(r, c) - mean2
            acc = acc + jnp.sum((v * v).reshape(CHUNK // 8, 8, CP), axis=0)
        return acc

    devs2 = lax.fori_loop(0, rows, dev_body, jnp.zeros((8, CP), F32))
    stat2[0, 0:1, :] = mean2
    stat2[0, 1:2, :] = jnp.sum(devs2, axis=0, keepdims=True)
    stat2_copies = send_stats(stat2, s2s, s2r)
    for copy in w2_copies:
        copy.wait()
    for copy in stat2_copies:
        copy.wait_recv()
    m2, a2 = combine(stat2)

    def second_body(r, _):
        for c in range(0, width, CHUNK):
            act[pl.ds(8 + c, CHUNK), :] = silu_half((row_chunk(r, c) - m2) * a2)
        spread_row(r + 1)
        return 0

    lax.fori_loop(0, rows, second_body, 0)

    def out_copy(r):
        return pltpu.make_async_copy(outbuf.at[r], out_ref.at[0, r], out_sem.at[r])

    def final_row(r):
        outbuf[r] = (lat[1 + r].astype(F32) + conv(r, w2, 0, C)).astype(BF16)

    def final_inner(r, _):
        final_row(r)
        out_copy(r).start()
        return 0

    lax.fori_loop(1, rows - 1, final_inner, 0)

    def halo_row(k, r):
        off = murecv[k][0:1] - m2
        for c in range(0, width, CHUNK):
            v = hrecv[k, pl.ds(c, CHUNK), :].astype(F32)
            act[pl.ds(8 + c, CHUNK), :] = silu_half((v + off) * a2)
        spread_row(r)

    @pl.when(me > 0)
    def _():
        for copy in halo_copies(1):
            copy.wait_recv()
        halo_row(0, 0)

    @pl.when(me < B - 1)
    def _():
        for copy in halo_copies(0):
            copy.wait_recv()
        halo_row(1, rows + 1)

    def final_edge(k, _):
        r = k * (rows - 1)
        final_row(r)
        out_copy(r).start()
        return 0

    lax.fori_loop(0, 2, final_edge, 0)

    for copy in stat1_copies + slot_copies + p1_copies + p2_copies + p3_copies + stat2_copies:
        copy.wait_send()

    @pl.when(me > 0)
    def _():
        up_copy().wait_send()
        for copy in halo_copies(0):
            copy.wait_send()

    @pl.when(me < B - 1)
    def _():
        down_copy().wait_send()
        for copy in halo_copies(1):
            copy.wait_send()

    for r in range(rows):
        out_copy(r).wait()


def block(mesh_shape, lat, temb, ra, stored_row, w1, down, up, w2, tp):
    B, R = mesh_shape["band"], mesh_shape["req"]
    _, rows, width, C = lat.shape
    rank = up.shape[1]
    tp = tp.T
    CP = round_up(C, LANES)
    piece = round_up(-(-(9 * C // 2 + 3 * rank) // B), 16)
    dims = (B, R, rows, width, C, rank, piece)
    ids = np.arange(CP) // (C // G)
    ok = np.arange(CP) < C
    gg = jnp.asarray((ids[:, None] == ids[None, :]) & ok[:, None] & ok[None, :], dtype=BF16)
    hbm = pl.BlockSpec(memory_space=pl.ANY)
    vmem = pl.BlockSpec(memory_space=pltpu.VMEM)
    smem = pl.BlockSpec(memory_space=pltpu.SMEM)
    V = pltpu.VMEM
    dma = lambda n: pltpu.SemaphoreType.DMA((n,))
    scratch = [
        V((rows + 2, width, C), BF16), V((width + 16, CP), F32), V((rows + 2, width, 1024), BF16),
        V((rows, width, CP), F32), V((3, 1024, C), BF16), V((3, 1024, C), BF16), V((3, 1024, LANES), BF16),
        V((64 + rank, CP), BF16), V(tp.shape, BF16), V(down.shape[1:], BF16), V(up.shape[1:], BF16), V((8, CP), F32),
        V((B, 8, CP), F32), V((B, 8, CP), F32), V((R, 8, LANES), jnp.int32), V((B * piece, LANES), BF16),
        V((B, piece, LANES), BF16), V((R, piece, LANES), BF16), V((R, piece, LANES), BF16), V((B, piece, LANES), BF16),
        V((2, width, CP), BF16), V((2, width, CP), BF16), V((2, 8, CP), F32), V((2, 8, CP), F32), V((rows, width, C), BF16),
        dma(4), dma(18), dma(18), dma(rows),
        dma(B), dma(B), dma(B), dma(B), dma(R), dma(R), dma(B), dma(B), dma(R), dma(R), dma(B), dma(B),
        dma(2), dma(2), dma(2), dma(2), dma(2), dma(2),
    ]
    return pl.pallas_call(
        functools.partial(kernel, dims),
        out_shape=jax.ShapeDtypeStruct(lat.shape, BF16),
        in_specs=[hbm, vmem, smem, smem, hbm, hbm, hbm, hbm, hbm, vmem],
        out_specs=hbm,
        scratch_shapes=scratch,
        compiler_params=pltpu.CompilerParams(
            collective_id=0, has_side_effects=True, vmem_limit_bytes=48 * 1024 * 1024),
        name="block",
    )(lat, temb, ra, stored_row, w1, down, up, w2, tp, gg)


def solution(mesh):
    in_specs = (
        P("req", "band", None, None),
        P("req", None),
        P("req", None),
        P(),
        P(),
        P(("band", "req"), None, None, None, None),
        P(("band", "req"), None, None),
        P(),
        P(),
    )
    return jax.shard_map(
        functools.partial(block, dict(mesh.shape)), mesh=mesh, in_specs=in_specs,
        out_specs=P("req", "band", None, None), check_vma=False)
```
